32 devices in a mesh: dp: 4 (over x, core), seq: 4 (over z), head: 2 (over y).
Axes of the slice: x: 2, y: 2, z: 4, core: 2. Of those that a mesh axis runs over, the one named last changes fastest.
Arguments:
- doc_ids: int32 [4096], P(('dp', 'seq')), parts along dimension 0, may hold values from 0 to 7, never falling along the last dimension, each value on 1 to 512 neighbouring positions
- light_q: bfloat16 [4096, 4096], P(('dp', 'seq'), 'head'), parts along dimension 0, may hold values from -0.59765625 to 0.59765625
- light_k: bfloat16 [4096, 4096], P(('dp', 'seq'), 'head'), parts along dimension 0, may hold values from -0.59765625 to 0.59765625
- light_v: bfloat16 [4096, 4096], P(('dp', 'seq'), 'head'), parts along dimension 0, may hold values from -6 to 6
- light_decay: float32 [32], P('head'), may hold values from 0 to 1
- light_grad_out: bfloat16 [4096, 4096], P(('dp', 'seq'), 'head'), parts along dimension 0, may hold values from -6 to 6
- soft_q: bfloat16 [4096, 4096], P(('dp', 'seq'), 'head'), parts along dimension 0, may hold values from -40 to 40
- soft_k: bfloat16 [4096, 4096], P(('dp', 'seq'), 'head'), parts along dimension 0, may hold values from -40 to 40
- soft_v: bfloat16 [4096, 4096], P(('dp', 'seq'), 'head'), parts along dimension 0, may hold values from -6 to 6
- soft_grad_out: bfloat16 [4096, 4096], P(('dp', 'seq'), 'head'), parts along dimension 0, may hold values from -6 to 6
Outputs:
- lightning_output: bfloat16 [4096, 4096], P(('dp', 'seq'), 'head'), parts along dimension 0
- lightning_query_gradient: bfloat16 [4096, 4096], P(('dp', 'seq'), 'head'), parts along dimension 0
- lightning_key_gradient: bfloat16 [4096, 4096], P(('dp', 'seq'), 'head'), parts along dimension 0
- lightning_value_gradient: bfloat16 [4096, 4096], P(('dp', 'seq'), 'head'), parts along dimension 0
- soft_out: bfloat16 [4096, 4096], P(('dp', 'seq'), 'head'), parts along dimension 0
- soft_dq: bfloat16 [4096, 4096], P(('dp', 'seq'), 'head'), parts along dimension 0
- soft_dk: bfloat16 [4096, 4096], P(('dp', 'seq'), 'head'), parts along dimension 0
- soft_dv: bfloat16 [4096, 4096], P(('dp', 'seq'), 'head'), parts along dimension 0
The draws below stay inside these ranges and needn't reach their ends.
There are 4 independent parts, one for each index of `dp`. The reference program is written for one: setup_inputs(seed, part) draws one part's arguments, and reference() takes and returns one part's arrays. A program takes and returns all parts, laid end to end along the dimension named above; an argument that names none is the same for every part. Nothing has to cross between parts.
Inputs may be any that keep to these rules, and one draw needn't show every extreme that they name: `doc_ids`: document ids never fall along the sequence; each document holds at most 512 tokens, and one holds exactly that many.
All inputs are finite; a program needn't handle non-finite values.
Results may differ from the reference program's by a relative error of at most 0.02.
Values may be sent and summed in bfloat16 or wider, within the bound.
A program may use at most 128 MiB of HBM per device.

```python
import math
import jax
import jax.numpy as jnp
import numpy as np
from jax import lax

H = 32
HD = 128
DOCS = 8
TOKENS = 1024


def draw_light_decay(key, part):
    base = jax.random.fold_in(key, 5309)
    slow_flag = jax.random.randint(jax.random.fold_in(base, 1), (H,), 0, 2) == 1
    slow_rate = jnp.exp(jax.random.uniform(jax.random.fold_in(base, 2), (H,), jnp.float32, math.log(1.0 / (16.0 * TOKENS)), math.log(1.0 / (4.0 * TOKENS))))
    fast_rate = jnp.exp(jax.random.uniform(jax.random.fold_in(base, 3), (H,), jnp.float32, math.log(1.0 / 50.0), math.log(1.0 / 20.0)))
    return jnp.where(slow_flag, slow_rate, fast_rate).astype(jnp.float32)


def soft_pair(key):
    base = jax.random.fold_in(key, 7103)
    query = jax.random.normal(jax.random.fold_in(base, 1), (TOKENS, H, HD), jnp.float32)
    keys = jax.random.normal(jax.random.fold_in(base, 2), (TOKENS, H, HD), jnp.float32)
    return (query.reshape(TOKENS, H * HD), keys.reshape(TOKENS, H * HD))


def draw_soft_q(key, part):
    return soft_pair(key)[0].astype(jnp.bfloat16)


def draw_soft_k(key, part):
    return soft_pair(key)[1].astype(jnp.bfloat16)


def levels(own_key, extent, shards, least, high):
    loudness = 1.0
    for axis_at, blocks in shards:
        draws = jax.random.uniform(jax.random.fold_in(jax.random.fold_in(own_key, 6), axis_at), (blocks,), jnp.float32, least / len(shards), high / len(shards))
        loudness = loudness * jnp.repeat(jnp.exp(draws), extent[axis_at] // blocks).reshape((-1,) + (1,) * (len(extent) - 1 - axis_at))
    return loudness


def split_up(amount, total, reach, lean):
    weights = [(1 << 20) // math.isqrt(standing ** lean) + 1 for standing in range(2, amount + 1)]
    spare, counts = total - reach - (amount - 1), [1] * (amount - 1)
    while spare > 0:
        movable = [i for i in range(amount - 1) if counts[i] < reach]
        whole, left = sum([weights[i] for i in movable]), spare
        for i in movable:
            more = min(reach - counts[i], max(1, left * weights[i] // whole), spare)
            counts[i] = counts[i] + more
            spare = spare - more
    return np.array([reach] + counts)


def ragged(own_key, number_of, total, bound, lean):
    if number_of == 2:
        one = jax.random.randint(own_key, (), max(1, total - bound), min(bound, total - 1) + 1)
        return jnp.stack([one, total - one])
    sizes = jnp.asarray(split_up(number_of, total, bound, lean), jnp.int32)
    twos = (number_of - 1) // 2
    source_of, receiver = sizes[1:1 + 2 * twos:2], sizes[2:2 + 2 * twos:2]
    room = jnp.minimum(source_of - 1, bound - receiver)
    moved = jax.random.randint(jax.random.fold_in(own_key, 1), (twos,), 0, 1 << 20) % (room + 1)
    sizes = sizes.at[1:1 + 2 * twos:2].set(source_of - moved).at[2:2 + 2 * twos:2].set(receiver + moved)
    return sizes[jax.random.permutation(jax.random.fold_in(own_key, 2), number_of)]


def bell_draw(own_key, dims, deviation, limit, split=(), kind=jnp.bfloat16):
    gain = levels(own_key, dims, split, -0.22, 0.18) if split else 1.0
    result = jax.random.normal(own_key, dims, jnp.float32) * deviation * gain
    return jnp.minimum(jnp.maximum(result, -limit), limit).astype(kind)


def setup_inputs(seed: int = 0, part: int = 0) -> dict:
    key_list = jax.random.split(jax.random.key(seed), 11)
    part_splits = jax.random.split(jax.random.fold_in(key_list[10], part), 11)
    return {
        "doc_ids": jnp.searchsorted(jnp.cumsum(ragged(part_splits[0], DOCS, TOKENS, TOKENS // 2, 2)), jnp.arange(TOKENS), side="right").astype(jnp.int32),
        "light_q": bell_draw(part_splits[1], (TOKENS, H * HD), 0.1, 0.59765625, ((0, 4), (1, 2))),
        "light_k": bell_draw(part_splits[2], (TOKENS, H * HD), 0.1, 0.59765625, ((0, 4), (1, 2))),
        "light_v": bell_draw(part_splits[3], (TOKENS, H * HD), 1.0, 6.0, ((0, 4), (1, 2))),
        "light_decay": draw_light_decay(jax.random.fold_in(key_list[10], 71), part),
        "light_grad_out": bell_draw(part_splits[5], (TOKENS, H * HD), 1.0, 6.0, ((0, 4), (1, 2))),
        "soft_q": draw_soft_q(jax.random.fold_in(jax.random.fold_in(key_list[10], part), 71), part),
        "soft_k": draw_soft_k(jax.random.fold_in(jax.random.fold_in(key_list[10], part), 71), part),
        "soft_v": bell_draw(part_splits[8], (TOKENS, H * HD), 1.0, 6.0, ((0, 4), (1, 2))),
        "soft_grad_out": bell_draw(part_splits[9], (TOKENS, H * HD), 1.0, 6.0, ((0, 4), (1, 2))),
    }


HIGHEST = lax.Precision.HIGHEST


def split_heads(whole):
    return jnp.transpose(whole.reshape(TOKENS, H, HD), (1, 0, 2))


def join_heads(parted):
    return jnp.transpose(parted, (1, 0, 2)).reshape(TOKENS, H * HD)


def reference(doc_ids, light_q, light_k, light_v, light_decay, light_grad_out, soft_q, soft_k, soft_v, soft_grad_out):
    order = jnp.arange(TOKENS, dtype=jnp.int32)
    allowed = (order[None, :] <= order[:, None]) & (doc_ids[None, :] == doc_ids[:, None])
    distance = jnp.maximum(order[:, None] - order[None, :], 0).astype(jnp.float32)
    scale = HD ** -0.5

    def light_head(inputs):
        query_half_rows, key_half_rows, value_half_rows, backward_sequence_share, slope = inputs
        query = query_half_rows.astype(jnp.float32)
        keys = key_half_rows.astype(jnp.float32)
        values = value_half_rows.astype(jnp.float32)
        grads = backward_sequence_share.astype(jnp.float32)
        weight = jnp.where(allowed, jnp.exp(-slope * distance), 0.0)
        scores = jnp.dot(query_half_rows, key_half_rows.T, preferred_element_type=jnp.float32) * weight
        output = jnp.dot(scores, values, precision=HIGHEST)
        grad_scores = jnp.dot(backward_sequence_share, value_half_rows.T, preferred_element_type=jnp.float32) * weight
        dquery = jnp.dot(grad_scores, keys, precision=HIGHEST)
        dkeys = jnp.dot(grad_scores.T, query, precision=HIGHEST)
        derivative_wrt_payloads = jnp.dot(scores.T, grads, precision=HIGHEST)
        return (output.astype(jnp.bfloat16), dquery.astype(jnp.bfloat16),
                dkeys.astype(jnp.bfloat16), derivative_wrt_payloads.astype(jnp.bfloat16))

    def soft_head(inputs):
        query, keys, values, grads = inputs
        logits = jnp.dot(query, keys.T, preferred_element_type=jnp.float32) * scale
        masked = jnp.where(allowed, logits, -1e30)
        top = jnp.max(masked, axis=1)
        raw = jnp.where(allowed, jnp.exp(masked - top[:, None]), 0.0)
        total = jnp.sum(raw, axis=1)
        expo = raw.astype(jnp.bfloat16)
        output = (jnp.dot(expo, values, preferred_element_type=jnp.float32) / total[:, None]).astype(jnp.bfloat16)
        lse = top + jnp.log(total)
        prob = jnp.where(allowed, jnp.exp(jnp.where(allowed, logits - lse[:, None], -1e30)), 0.0)
        attention_weights_bfloat16 = prob.astype(jnp.bfloat16)
        delta = jnp.sum(grads.astype(jnp.float32) * output.astype(jnp.float32), axis=1)
        derivative_wrt_payloads = jnp.dot(attention_weights_bfloat16.T, grads, preferred_element_type=jnp.float32)
        dprob = jnp.dot(grads, values.T, preferred_element_type=jnp.float32)
        dlogit = (prob * (dprob - delta[:, None])).astype(jnp.bfloat16)
        dquery = jnp.dot(dlogit, keys, preferred_element_type=jnp.float32) * scale
        dkeys = jnp.dot(dlogit.T, query, preferred_element_type=jnp.float32) * scale
        return (output, dquery.astype(jnp.bfloat16), dkeys.astype(jnp.bfloat16), derivative_wrt_payloads.astype(jnp.bfloat16))

    light = lax.map(light_head, (split_heads(light_q), split_heads(light_k), split_heads(light_v),
                                 split_heads(light_grad_out), light_decay))
    soft = lax.map(soft_head, (split_heads(soft_q), split_heads(soft_k), split_heads(soft_v),
                               split_heads(soft_grad_out)))
    return (join_heads(light[0]), join_heads(light[1]), join_heads(light[2]), join_heads(light[3]),
            join_heads(soft[0]), join_heads(soft[1]), join_heads(soft[2]), join_heads(soft[3]))
```

```python
import functools
import math

import jax
import jax.numpy as jnp
from jax import lax
from jax.experimental import pallas as pl
from jax.experimental.pallas import tpu as pltpu
from jax.sharding import PartitionSpec as P

NEG = -1e30
F32 = jnp.float32
BF16 = jnp.bfloat16
VMEM_LIMIT = 50 * 1024 * 1024


def mm(a, b, ca, cb):
    return lax.dot_general(a, b, (((ca,), (cb,)), ((), ())), preferred_element_type=F32)


def shift(value, axis, steps):
    count = lax.axis_size(axis)
    first, last = (max(0, -steps), min(count, count - steps))
    return lax.ppermute(value, axis, [(source, source + steps) for source in range(first, last)])


def relay(value, axis, steps, reach):
    got = []
    for _ in range(reach):
        value = shift(value, axis, steps)
        got.append(value)
    return got


def state_kernel(hb, width, decay, ids_col, q, k, v, g, ahead, back):
    rows = q.shape[0]
    base = pl.program_id(0) * hb
    ids = ids_col[...]
    pos = lax.broadcasted_iota(jnp.int32, (rows, width), 0).astype(F32)
    head_on = jnp.where(ids == ids_col[0:1, :], 0.0, NEG)
    tail_on = jnp.where(ids == ids_col[rows - 1 : rows, :], 0.0, NEG)
    for h in range(hb):
        lam = decay[base + h]
        cols = slice(h * width, (h + 1) * width)
        to_end = jnp.exp(tail_on - lam * (rows - 1.0 - pos))
        since = jnp.exp(head_on - lam * (pos + 1.0))
        kd = (k[:, cols].astype(F32) * to_end).astype(BF16)
        qd = (q[:, cols].astype(F32) * since).astype(BF16)
        ahead[h] = mm(kd, v[:, cols], 0, 0).astype(BF16)
        back[h] = mm(qd, g[:, cols], 0, 0).astype(BF16)


def light_kernel(hb, width, reach, decay, coef_f, coef_b, ids_col, ids_row, q, k, v, g, *rest):
    states_f, states_b = rest[:reach], rest[reach : 2 * reach]
    out, dq, dk, dv, bias, dist = rest[2 * reach :]
    rows = q.shape[0]
    base = pl.program_id(0) * hb
    ids = ids_col[...]

    @pl.when(pl.program_id(0) == 0)
    def _():
        t = lax.broadcasted_iota(jnp.int32, (rows, rows), 0)
        s = lax.broadcasted_iota(jnp.int32, (rows, rows), 1)
        bias[...] = jnp.where((ids == ids_row[...]) & (s <= t), 0.0, NEG)
        dist[...] = jnp.maximum(t - s, 0).astype(F32)

    pos = lax.broadcasted_iota(jnp.int32, (rows, width), 0).astype(F32)
    head_on = jnp.where(ids == ids_col[0:1, :], 0.0, NEG)
    tail_on = jnp.where(ids == ids_col[rows - 1 : rows, :], 0.0, NEG)
    for h in range(hb):
        lam = decay[base + h]
        cols = slice(h * width, (h + 1) * width)
        qh, kh, vh, gh = q[:, cols], k[:, cols], v[:, cols], g[:, cols]
        state = coef_f[0, base + h] * states_f[0][h].astype(F32)
        later = coef_b[0, base + h] * states_b[0][h].astype(F32)
        for d in range(1, reach):
            state = state + coef_f[d, base + h] * states_f[d][h].astype(F32)
            later = later + coef_b[d, base + h] * states_b[d][h].astype(F32)
        state, later = state.astype(BF16), later.astype(BF16)
        to_end = jnp.exp(tail_on - lam * (rows - 1.0 - pos))
        since = jnp.exp(head_on - lam * (pos + 1.0))
        weight = jnp.exp(bias[...] - lam * dist[...])
        scores = (mm(qh, kh, 1, 1) * weight).astype(BF16)
        grads = (mm(gh, vh, 1, 1) * weight).astype(BF16)
        out[:, cols] = (mm(scores, vh, 1, 0) + mm(qh, state, 1, 0) * since).astype(BF16)
        dq[:, cols] = (mm(grads, kh, 1, 0) + mm(gh, state, 1, 1) * since).astype(BF16)
        dk[:, cols] = (mm(grads, qh, 0, 0) + mm(vh, later, 1, 1) * to_end).astype(BF16)
        dv[:, cols] = (mm(scores, gh, 0, 0) + mm(kh, later, 1, 0) * to_end).astype(BF16)


def query_kernel(hb, width, reach, fresh, ids_col, ids_row, q, g, k0, v0, *rest):
    far, rest = rest[:reach], rest[reach:]
    out, dq, stat, bias = rest if fresh else rest[2:]
    rows = q.shape[0]
    scale = width ** -0.5

    @pl.when(pl.program_id(0) == 0)
    def _():
        ids = ids_col[...]
        t = lax.broadcasted_iota(jnp.int32, (rows, rows), 0)
        s = lax.broadcasted_iota(jnp.int32, (rows, rows), 1)
        for d in range(reach + 1):
            same = ids == ids_row[:, d * rows : (d + 1) * rows]
            if d == 0:
                same = same & (s <= t)
            bias[d] = jnp.where(same, 0.0, NEG)

    lane = lax.broadcasted_iota(jnp.int32, (rows, width), 1)
    for h in range(hb):
        cols = slice(h * width, (h + 1) * width)
        qh, gh = q[:, cols], g[:, cols]
        keys = [k0[:, cols]] + [m[0, :, cols] for m in far]
        values = [v0[:, cols]] + [m[1, :, cols] for m in far]
        raw = [mm(qh, kh, 1, 1) + bias[d] for d, kh in enumerate(keys)]
        top = functools.reduce(jnp.maximum, raw).max(axis=1, keepdims=True)
        expo = [jnp.exp2((r - top) * (scale * math.log2(math.e))) for r in raw]
        total = functools.reduce(jnp.add, expo).sum(axis=1, keepdims=True)
        acc = functools.reduce(
            jnp.add, [mm(e.astype(BF16), vh, 1, 0) for e, vh in zip(expo, values)]
        )
        inv = 1.0 / total
        o16 = (acc * inv).astype(BF16)
        out[:, cols] = o16
        delta = (gh.astype(F32) * o16.astype(F32)).sum(axis=1, keepdims=True)
        lse = top + jnp.log(total) * (1.0 / scale)
        acc = None
        for e, kh, vh in zip(expo, keys, values):
            ds = ((e * inv) * (mm(gh, vh, 1, 1) - delta)).astype(BF16)
            part = mm(ds, kh, 1, 0)
            acc = part if acc is None else acc + part
        dq[:, cols] = (acc * scale).astype(BF16)
        stat[h] = jnp.where(lane == 0, lse, delta).T[0:2, :]


def key_kernel(hb, width, reach, fresh, ids_col, ids_row, k, v, q0, g0, stat0, *rest):
    far, stats, rest = rest[:reach], rest[reach : 2 * reach], rest[2 * reach :]
    dk, dv, bias = rest if fresh else rest[2:]
    rows = k.shape[0]
    scale = width ** -0.5

    @pl.when(pl.program_id(0) == 0)
    def _():
        ids = ids_col[...]
        s = lax.broadcasted_iota(jnp.int32, (rows, rows), 0)
        t = lax.broadcasted_iota(jnp.int32, (rows, rows), 1)
        for d in range(reach + 1):
            same = ids == ids_row[:, d * rows : (d + 1) * rows]
            if d == 0:
                same = same & (s <= t)
            bias[d] = jnp.where(same, 0.0, NEG)

    for h in range(hb):
        cols = slice(h * width, (h + 1) * width)
        kh, vh = k[:, cols], v[:, cols]
        dk_acc = dv_acc = None
        for d in range(reach + 1):
            qh = q0[:, cols] if d == 0 else far[d - 1][0, :, cols]
            gh = g0[:, cols] if d == 0 else far[d - 1][1, :, cols]
            st = stat0[h] if d == 0 else stats[d - 1][h]
            lse, delta = st[0:1, :], st[1:2, :]
            raw = mm(kh, qh, 1, 1) + bias[d]
            prob = jnp.exp2((raw - lse) * (scale * math.log2(math.e)))
            ds = (prob * (mm(vh, gh, 1, 1) - delta)).astype(BF16)
            dv_part = mm(prob.astype(BF16), gh, 1, 0)
            dk_part = mm(ds, qh, 1, 0)
            dk_acc = dk_part if dk_acc is None else dk_acc + dk_part
            dv_acc = dv_part if dv_acc is None else dv_acc + dv_part
        dk[:, cols] = (dk_acc * scale).astype(BF16)
        dv[:, cols] = dv_acc.astype(BF16)


def per_device(
    doc_ids,
    light_q,
    light_k,
    light_v,
    light_decay,
    light_grad_out,
    soft_q,
    soft_k,
    soft_v,
    soft_grad_out,
):
    rows, cols = light_q.shape
    heads = light_decay.shape[0]
    width = cols // heads
    shards = lax.axis_size("seq")
    total_rows = rows * shards
    reach = min(shards - 1, (rows + total_rows // 2 - 2) // rows)
    groups = 4 if heads % 4 == 0 else 1
    per_group = heads // groups
    hb = 2 if per_group % 2 == 0 else 1
    if reach > 2:
        hb = 1
    gw = per_group * width
    steps = per_group // hb
    bw = hb * width
    full = jax.ShapeDtypeStruct((rows, cols), BF16)
    params = pltpu.CompilerParams(vmem_limit_bytes=VMEM_LIMIT)
    smem = pl.BlockSpec(memory_space=pltpu.SMEM)

    def whole(shape):
        return pl.BlockSpec(shape, lambda i: (0,) * len(shape))

    ids = doc_ids + 1
    ids_before = relay(ids, "seq", 1, reach)
    ids_after = relay(ids, "seq", -1, reach)

    def cut(a, g):
        return a[:, g * gw : (g + 1) * gw]

    before, after = [], []
    for g in range(groups):
        before.append(relay(jnp.stack([cut(soft_k, g), cut(soft_v, g)]), "seq", 1, reach))
        after.append(relay(jnp.stack([cut(soft_q, g), cut(soft_grad_out, g)]), "seq", -1, reach))

    ids_col = ids[:, None]
    row_before = jnp.concatenate([ids] + ids_before)[None, :]
    row_after = jnp.concatenate([ids] + ids_after)[None, :]
    col_spec = whole((rows, 1))
    row_spec = whole((1, rows * (reach + 1)))

    lhb = hb
    lspec = pl.BlockSpec((rows, lhb * width), lambda i: (0, i))
    sspec = pl.BlockSpec((lhb, width, width), lambda i: (i, 0, 0))
    state_shape = jax.ShapeDtypeStruct((heads, width, width), BF16)
    state, pending = pl.pallas_call(
        functools.partial(state_kernel, lhb, width),
        grid=(heads // lhb,),
        in_specs=[smem, col_spec] + [lspec] * 4,
        out_specs=[sspec] * 2,
        out_shape=[state_shape] * 2,
        compiler_params=params,
        cost_estimate=pl.CostEstimate(
            flops=4 * rows * width * cols, bytes_accessed=10 * rows * cols, transcendentals=0
        ),
        name="light_states",
    )(light_decay, ids_col, light_q, light_k, light_v, light_grad_out)
    states_f = relay(state, "seq", 1, reach)
    states_b = relay(pending, "seq", -1, reach)
    lap = jnp.arange(reach, dtype=F32)[:, None]
    keep = jnp.exp(-light_decay[None, :] * (lap * rows))
    gate_f = jnp.stack([a[-1] == ids[0] for a in ids_before])
    gate_b = jnp.stack([a[0] == ids[-1] for a in ids_after])
    coef_f = jnp.where(gate_f[:, None], keep, 0.0)
    coef_b = jnp.where(gate_b[:, None], keep, 0.0)
    light = pl.pallas_call(
        functools.partial(light_kernel, lhb, width, reach),
        grid=(heads // lhb,),
        in_specs=[smem] * 3
        + [col_spec, whole((1, rows))]
        + [lspec] * 4
        + [sspec] * (2 * reach),
        out_specs=[lspec] * 4,
        out_shape=[full] * 4,
        scratch_shapes=[pltpu.VMEM((rows, rows), F32)] * 2,
        compiler_params=params,
        cost_estimate=pl.CostEstimate(
            flops=24 * rows * rows * cols, bytes_accessed=16 * rows * cols, transcendentals=0
        ),
        name="light",
    )(
        light_decay,
        coef_f,
        coef_b,
        ids_col,
        ids[None, :],
        light_q,
        light_k,
        light_v,
        light_grad_out,
        *states_f,
        *states_b,
    )

    bias = pltpu.VMEM((reach + 1, rows, rows), F32)
    far_spec = pl.BlockSpec((2, rows, bw), lambda i: (0, 0, i))
    stat_spec = pl.BlockSpec((hb, 2, rows), lambda i: (i, 0, 0))
    anywhere = pl.BlockSpec(memory_space=pl.ANY)
    cost = pl.CostEstimate(
        flops=24 * (reach + 1) * rows * rows * gw,
        bytes_accessed=(16 + 4 * reach) * rows * gw,
        transcendentals=0,
    )
    held, stats = (), []
    for g in range(groups):
        own = pl.BlockSpec((rows, bw), lambda i, g=g: (0, g * steps + i))
        fixed = 6 + reach
        *held, stat = pl.pallas_call(
            functools.partial(query_kernel, hb, width, reach, g == 0),
            grid=(steps,),
            in_specs=[col_spec, row_spec] + [own] * 4 + [far_spec] * reach + [anywhere] * len(held),
            out_specs=[own, own, stat_spec],
            out_shape=[full, full, jax.ShapeDtypeStruct((per_group, 2, rows), F32)],
            scratch_shapes=[bias],
            input_output_aliases={} if g == 0 else {fixed: 0, fixed + 1: 1},
            compiler_params=params,
            cost_estimate=cost,
            name="soft_queries",
        )(ids_col, row_before, soft_q, soft_grad_out, soft_k, soft_v, *before[g], *held)
        stats.append([stat] + relay(stat, "seq", -1, reach))
    soft_out, soft_dq = held
    held = ()
    for g in range(groups):
        own = pl.BlockSpec((rows, bw), lambda i, g=g: (0, g * steps + i))
        fixed = 7 + 2 * reach
        held = pl.pallas_call(
            functools.partial(key_kernel, hb, width, reach, g == 0),
            grid=(steps,),
            in_specs=[col_spec, row_spec]
            + [own] * 4
            + [stat_spec]
            + [far_spec] * reach
            + [stat_spec] * reach
            + [anywhere] * len(held),
            out_specs=[own, own],
            out_shape=[full, full],
            scratch_shapes=[bias],
            input_output_aliases={} if g == 0 else {fixed: 0, fixed + 1: 1},
            compiler_params=params,
            cost_estimate=cost,
            name="soft_keys",
        )(
            ids_col,
            row_after,
            soft_k,
            soft_v,
            soft_q,
            soft_grad_out,
            stats[g][0],
            *after[g],
            *stats[g][1:],
            *held,
        )
    soft_dk, soft_dv = held
    return (*light, soft_out, soft_dq, soft_dk, soft_dv)


def solution(mesh):
    wide = P(("dp", "seq"), "head")
    return jax.shard_map(
        per_device,
        mesh=mesh,
        in_specs=(P(("dp", "seq")), wide, wide, wide, P("head"), wide, wide, wide, wide, wide),
        out_specs=(wide,) * 8,
        check_vma=False,
    )
```

```python
import functools
import math

import jax
import jax.numpy as jnp
from jax import lax
from jax.experimental import pallas as pl
from jax.experimental.pallas import tpu as pltpu
from jax.sharding import PartitionSpec as P

NEG = -1e30
F32 = jnp.float32
BF16 = jnp.bfloat16
VMEM_LIMIT = 50 * 1024 * 1024


def mm(a, b, ca, cb):
    return lax.dot_general(a, b, (((ca,), (cb,)), ((), ())), preferred_element_type=F32)


def attention_kernel(
    shards,
    reach,
    heads,
    hb,
    decay,
    ids_col,
    ids_row,
    lq,
    lk,
    lv,
    lg,
    sq,
    sk,
    sv,
    sg,
    l_out,
    l_dq,
    l_dk,
    l_dv,
    s_out,
    s_dq,
    s_dk,
    s_dv,
    slots,
    states,
    own_states,
    stats,
    own_stats,
    ids_slots,
    bias_q,
    bias_k,
    dist,
    send_sem,
    recv_sem,
    state_send,
    state_recv,
    stat_send,
    stat_recv,
    ids_send,
    ids_recv,
):
    rows, all_cols = lq.shape
    width = all_cols // heads
    chunks = heads // hb
    cw = hb * width
    me = lax.axis_index("seq")
    scale = width ** -0.5
    unit = scale * math.log2(math.e)
    wide_own = (sk, sv, sq, sg)
    way_of = (1, 1, -1, -1)

    def col(c, n=None):
        n = cw if n is None else n
        return pl.ds(pl.multiple_of(c * n, n), n)

    def sends(way, hop):
        if way > 0:
            return (me >= hop) & (me + 1 < shards)
        return (me + hop < shards) & (me >= 1)

    def takes(way, hop):
        return me >= hop + 1 if way > 0 else me + hop + 1 < shards

    def wide_copy(kind, hop, c):
        source = wide_own[kind].at[:, col(c)] if hop == 0 else slots.at[kind, hop - 1, :, col(c)]
        return pltpu.make_async_remote_copy(
            src_ref=source,
            dst_ref=slots.at[kind, hop, :, col(c)],
            send_sem=send_sem.at[kind, hop, c],
            recv_sem=recv_sem.at[kind, hop, c],
            device_id={"seq": me + way_of[kind]},
            device_id_type=pl.DeviceIdType.MESH,
        )

    def state_copy(kind, hop, c):
        part = pl.ds(c * hb, hb)
        source = own_states.at[kind, part] if hop == 0 else states.at[kind, hop - 1, part]
        return pltpu.make_async_remote_copy(
            src_ref=source,
            dst_ref=states.at[kind, hop, part],
            send_sem=state_send.at[kind, hop, c],
            recv_sem=state_recv.at[kind, hop, c],
            device_id={"seq": me + (1, -1)[kind]},
            device_id_type=pl.DeviceIdType.MESH,
        )

    def stat_copy(hop, c):
        part = pl.ds(c * hb, hb)
        source = own_stats.at[part] if hop == 0 else stats.at[hop - 1, part]
        return pltpu.make_async_remote_copy(
            src_ref=source,
            dst_ref=stats.at[hop, part],
            send_sem=stat_send.at[hop, c],
            recv_sem=stat_recv.at[hop, c],
            device_id={"seq": me - 1},
            device_id_type=pl.DeviceIdType.MESH,
        )

    def ids_copy(kind, hop):
        return pltpu.make_async_remote_copy(
            src_ref=ids_row if hop == 0 else ids_slots.at[kind, hop - 1],
            dst_ref=ids_slots.at[kind, hop],
            send_sem=ids_send.at[kind, hop],
            recv_sem=ids_recv.at[kind, hop],
            device_id={"seq": me + (1, -1)[kind]},
            device_id_type=pl.DeviceIdType.MESH,
        )

    def start_wide(hop, c):
        for way, kinds in ((1, (0, 1)), (-1, (2, 3))):

            @pl.when(sends(way, hop))
            def _():
                for kind in kinds:
                    wide_copy(kind, hop, c).start()

    def start_states(hop, c):
        for kind, way in enumerate((1, -1)):

            @pl.when(sends(way, hop))
            def _():
                state_copy(kind, hop, c).start()

    def await_chunk(hop, c):
        for way, kinds in ((1, (0, 1)), (-1, (2, 3))):

            @pl.when(takes(way, hop))
            def _():
                for kind in kinds:
                    wide_copy(kind, hop, c).wait_recv()
                state_copy(0 if way > 0 else 1, hop, c).wait_recv()

    ids = ids_col[...]
    pos = lax.broadcasted_iota(jnp.int32, (rows, width), 0).astype(F32)
    lane = lax.broadcasted_iota(jnp.int32, (rows, width), 1)
    head_on = jnp.where(ids == ids_col[0:1, :], 0.0, NEG)
    tail_on = jnp.where(ids == ids_col[rows - 1 : rows, :], 0.0, NEG)

    def make_states(c):
        for j in range(hb):
            h = c * hb + j
            lam = decay[h]
            cols = col(h, width)
            to_end = jnp.exp(tail_on - lam * (rows - 1.0 - pos))
            since = jnp.exp(head_on - lam * (pos + 1.0))
            kd = (lk[:, cols].astype(F32) * to_end).astype(BF16)
            qd = (lq[:, cols].astype(F32) * since).astype(BF16)
            own_states[0, h] = mm(kd, lv[:, cols], 0, 0).astype(BF16)
            own_states[1, h] = mm(qd, lg[:, cols], 0, 0).astype(BF16)

    def light(c):
        for j in range(hb):
            h = c * hb + j
            lam = decay[h]
            cols = col(h, width)
            qh, kh, vh, gh = lq[:, cols], lk[:, cols], lv[:, cols], lg[:, cols]
            state = later = None
            for d in range(reach):
                keep = jnp.exp(jnp.zeros((1, width), F32) - lam * (rows * d))
                met = ids_slots[0, d, :, rows - 1 : rows] == ids_col[0:1, :]
                left = ids_slots[1, d, :, 0:1] == ids_col[rows - 1 : rows, :]
                ahead = jnp.where(met, keep, 0.0) * states[0, d, h].astype(F32)
                back = jnp.where(left, keep, 0.0) * states[1, d, h].astype(F32)
                state = ahead if state is None else state + ahead
                later = back if later is None else later + back
            state, later = state.astype(BF16), later.astype(BF16)
            to_end = jnp.exp(tail_on - lam * (rows - 1.0 - pos))
            since = jnp.exp(head_on - lam * (pos + 1.0))
            weight = jnp.exp(bias_q[0] - lam * dist[...])
            scores = (mm(qh, kh, 1, 1) * weight).astype(BF16)
            grads = (mm(gh, vh, 1, 1) * weight).astype(BF16)
            l_out[:, cols] = (mm(scores, vh, 1, 0) + mm(qh, state, 1, 0) * since).astype(BF16)
            l_dq[:, cols] = (mm(grads, kh, 1, 0) + mm(gh, state, 1, 1) * since).astype(BF16)
            l_dk[:, cols] = (mm(grads, qh, 0, 0) + mm(vh, later, 1, 1) * to_end).astype(BF16)
            l_dv[:, cols] = (mm(scores, gh, 0, 0) + mm(kh, later, 1, 0) * to_end).astype(BF16)

    def queries(c):
        for j in range(hb):
            h = c * hb + j
            cols = col(h, width)
            qh, gh = sq[:, cols], sg[:, cols]
            keys = [sk[:, cols]] + [slots[0, d, :, cols] for d in range(reach)]
            values = [sv[:, cols]] + [slots[1, d, :, cols] for d in range(reach)]
            raw = [mm(qh, kh, 1, 1) + bias_q[d] for d, kh in enumerate(keys)]
            top = functools.reduce(jnp.maximum, raw).max(axis=1, keepdims=True)
            expo = [jnp.exp2((r - top) * unit) for r in raw]
            total = functools.reduce(jnp.add, expo).sum(axis=1, keepdims=True)
            acc = functools.reduce(
                jnp.add, [mm(e.astype(BF16), vh, 1, 0) for e, vh in zip(expo, values)]
            )
            inv = 1.0 / total
            o16 = (acc * inv).astype(BF16)
            s_out[:, cols] = o16
            delta = (gh.astype(F32) * o16.astype(F32)).sum(axis=1, keepdims=True)
            lse = top + jnp.log(total) * (1.0 / scale)
            acc = None
            for e, kh, vh in zip(expo, keys, values):
                ds = ((e * inv) * (mm(gh, vh, 1, 1) - delta)).astype(BF16)
                part = mm(ds, kh, 1, 0)
                acc = part if acc is None else acc + part
            s_dq[:, cols] = (acc * scale).astype(BF16)
            own_stats[h] = jnp.where(lane == 0, lse, delta).T[0:8, :]

    def keys_side(c):
        for j in range(hb):
            h = c * hb + j
            cols = col(h, width)
            kh, vh = sk[:, cols], sv[:, cols]
            dk_acc = dv_acc = None
            for d in range(reach + 1):
                qh = sq[:, cols] if d == 0 else slots[2, d - 1, :, cols]
                gh = sg[:, cols] if d == 0 else slots[3, d - 1, :, cols]
                st = own_stats[h] if d == 0 else stats[d - 1, h]
                lse, delta = st[0:1, :], st[1:2, :]
                raw = mm(kh, qh, 1, 1) + bias_k[d]
                prob = jnp.exp2((raw - lse) * unit)
                ds = (prob * (mm(vh, gh, 1, 1) - delta)).astype(BF16)
                dv_part = mm(prob.astype(BF16), gh, 1, 0)
                dk_part = mm(ds, qh, 1, 0)
                dk_acc = dk_part if dk_acc is None else dk_acc + dk_part
                dv_acc = dv_part if dv_acc is None else dv_acc + dv_part
            s_dk[:, cols] = (dk_acc * scale).astype(BF16)
            s_dv[:, cols] = dv_acc.astype(BF16)

    barrier = pltpu.get_barrier_semaphore()
    for way, there in ((-1, me >= 1), (1, me + 1 < shards)):

        @pl.when(there)
        def _():
            pl.semaphore_signal(
                barrier, 1, device_id={"seq": me + way}, device_id_type=pl.DeviceIdType.MESH
            )

    pl.semaphore_wait(barrier, jnp.where((me == 0) | (me == shards - 1), 1, 2))

    for kind, way in enumerate((1, -1)):

        @pl.when(sends(way, 0))
        def _():
            ids_copy(kind, 0).start()

    start_wide(0, 0)
    make_states(0)
    start_states(0, 0)

    for d in range(reach):
        for way, kinds in ((1, (0, 1)), (-1, (2, 3))):

            @pl.when(jnp.logical_not(takes(way, d)))
            def _():
                for kind in kinds:
                    slots[kind, d] = jnp.zeros((rows, all_cols), BF16)
                one = kinds[0] // 2
                states[one, d] = jnp.zeros((heads, width, width), BF16)
                ids_slots[one, d] = jnp.zeros((1, rows), jnp.int32)
                if way < 0:
                    stats[d] = jnp.zeros((heads, 8, rows), F32)

    t = lax.broadcasted_iota(jnp.int32, (rows, rows), 0)
    s = lax.broadcasted_iota(jnp.int32, (rows, rows), 1)
    same = ids == ids_row[...]
    bias_q[0] = jnp.where(same & (s <= t), 0.0, NEG)
    bias_k[0] = jnp.where(same & (t <= s), 0.0, NEG)
    dist[...] = jnp.maximum(t - s, 0).astype(F32)
    for d in range(reach):
        for kind, way in enumerate((1, -1)):

            @pl.when(takes(way, d))
            def _():
                ids_copy(kind, d).wait_recv()

            if d + 1 < reach:

                @pl.when(sends(way, d + 1))
                def _():
                    ids_copy(kind, d + 1).start()

    for d in range(reach):
        bias_q[d + 1] = jnp.where(ids == ids_slots[0, d], 0.0, NEG)
        bias_k[d + 1] = jnp.where(ids == ids_slots[1, d], 0.0, NEG)

    def step(at, carry):
        @pl.when(at + 1 < chunks)
        def _():
            start_wide(0, at + 1)
            make_states(at + 1)
            start_states(0, at + 1)

        for d in range(reach - 1):

            @pl.when((at >= d) & (at - d < chunks))
            def _():
                await_chunk(d, at - d)
                start_wide(d + 1, at - d)
                start_states(d + 1, at - d)

        mid = at - (reach - 1)

        @pl.when((mid >= 0) & (mid < chunks))
        def _():
            await_chunk(reach - 1, mid)
            queries(mid)

            @pl.when(sends(-1, 0))
            def _():
                stat_copy(0, mid).start()

            light(mid)

        for d in range(reach - 1):

            @pl.when((mid >= d) & (mid - d < chunks))
            def _():
                @pl.when(takes(-1, d))
                def _():
                    stat_copy(d, mid - d).wait_recv()

                @pl.when(sends(-1, d + 1))
                def _():
                    stat_copy(d + 1, mid - d).start()

        last = mid - (reach - 1)

        @pl.when((last >= 0) & (last < chunks))
        def _():
            @pl.when(takes(-1, reach - 1))
            def _():
                stat_copy(reach - 1, last).wait_recv()

            keys_side(last)

        return carry

    lax.fori_loop(0, chunks + 2 * (reach - 1), step, 0)

    for hop in range(reach):
        for way, kinds in ((1, (0, 1)), (-1, (2, 3))):

            @pl.when(sends(way, hop))
            def _():
                one = kinds[0] // 2
                ids_copy(one, hop).wait_send()

                def drain(c, carry):
                    for kind in kinds:
                        wide_copy(kind, hop, c).wait_send()
                    state_copy(one, hop, c).wait_send()
                    if way < 0:
                        stat_copy(hop, c).wait_send()
                    return carry

                lax.fori_loop(0, chunks, drain, 0)


def per_device(doc_ids, light_q, light_k, light_v, light_decay, light_grad_out, *soft):
    rows, cols = light_q.shape
    heads = light_decay.shape[0]
    width = cols // heads
    shards = lax.axis_size("seq")
    total_rows = rows * shards
    reach = min(shards - 1, (rows + total_rows // 2 - 2) // rows)
    hb = 2 if heads % 2 == 0 else 1
    chunks = heads // hb
    ids = doc_ids + 1
    vmem = pl.BlockSpec(memory_space=pltpu.VMEM)
    dma = pltpu.SemaphoreType.DMA
    return pl.pallas_call(
        functools.partial(attention_kernel, shards, reach, heads, hb),
        in_specs=[pl.BlockSpec(memory_space=pltpu.SMEM)] + [vmem] * 10,
        out_specs=[vmem] * 8,
        out_shape=[jax.ShapeDtypeStruct((rows, cols), BF16)] * 8,
        scratch_shapes=[
            pltpu.VMEM((4, reach, rows, cols), BF16),
            pltpu.VMEM((2, reach, heads, width, width), BF16),
            pltpu.VMEM((2, heads, width, width), BF16),
            pltpu.VMEM((reach, heads, 8, rows), F32),
            pltpu.VMEM((heads, 8, rows), F32),
            pltpu.VMEM((2, reach, 1, rows), jnp.int32),
            pltpu.VMEM((reach + 1, rows, rows), F32),
            pltpu.VMEM((reach + 1, rows, rows), F32),
            pltpu.VMEM((rows, rows), F32),
            dma((4, reach, chunks)),
            dma((4, reach, chunks)),
            dma((2, reach, chunks)),
            dma((2, reach, chunks)),
            dma((reach, chunks)),
            dma((reach, chunks)),
            dma((2, reach)),
            dma((2, reach)),
        ],
        compiler_params=pltpu.CompilerParams(
            vmem_limit_bytes=VMEM_LIMIT, collective_id=0, has_side_effects=True
        ),
        cost_estimate=pl.CostEstimate(
            flops=40 * (reach + 1) * rows * rows * cols,
            bytes_accessed=32 * rows * cols,
            transcendentals=0,
        ),
        name="attention",
    )(light_decay, ids[:, None], ids[None, :], light_q, light_k, light_v, light_grad_out, *soft)


def solution(mesh):
    wide = P(("dp", "seq"), "head")
    return jax.shard_map(
        per_device,
        mesh=mesh,
        in_specs=(P(("dp", "seq")), wide, wide, wide, P("head"), wide, wide, wide, wide, wide),
        out_specs=(wide,) * 8,
        check_vma=False,
    )
```

```python
import functools
import math

import jax
import jax.numpy as jnp
from jax import lax
from jax.experimental import pallas as pl
from jax.experimental.pallas import tpu as pltpu
from jax.sharding import PartitionSpec as P

NEG = -1e30
F32 = jnp.float32
BF16 = jnp.bfloat16
VMEM_LIMIT = 60 * 1024 * 1024


def mm(a, b, ca, cb):
    return lax.dot_general(a, b, (((ca,), (cb,)), ((), ())), preferred_element_type=F32)


def attention_kernel(
    shards,
    reach,
    heads,
    hb,
    decay,
    ids_col,
    ids_row,
    lq,
    lk,
    lv,
    lg,
    sq,
    sk,
    sv,
    sg,
    l_out,
    l_dq,
    l_dk,
    l_dv,
    s_out,
    s_dq,
    s_dk,
    s_dv,
    slots,
    states,
    own_states,
    stats,
    own_stats,
    ids_slots,
    bias_q,
    bias_k,
    dist,
    send_sem,
    recv_sem,
    state_send,
    state_recv,
    stat_send,
    stat_recv,
    ids_send,
    ids_recv,
):
    rows, all_cols = lq.shape
    width = all_cols // heads
    chunks = heads // hb
    cw = hb * width
    me = lax.axis_index("seq")
    scale = width ** -0.5
    unit = scale * math.log2(math.e)
    wide_own = (sk, sv, sq, sg)
    way_of = (1, 1, -1, -1)

    def col(c, n=None):
        n = cw if n is None else n
        return pl.ds(pl.multiple_of(c * n, n), n)

    def sends(way, hop):
        if way > 0:
            return (me >= hop) & (me + 1 < shards)
        return (me + hop < shards) & (me >= 1)

    def takes(way, hop):
        return me >= hop + 1 if way > 0 else me + hop + 1 < shards

    def wide_copy(kind, hop, c):
        source = wide_own[kind].at[:, col(c)] if hop == 0 else slots.at[kind, hop - 1, :, col(c)]
        return pltpu.make_async_remote_copy(
            src_ref=source,
            dst_ref=slots.at[kind, hop, :, col(c)],
            send_sem=send_sem.at[kind, hop, c],
            recv_sem=recv_sem.at[kind, hop, c],
            device_id={"seq": me + way_of[kind]},
            device_id_type=pl.DeviceIdType.MESH,
        )

    def state_copy(kind, hop, c):
        part = pl.ds(c * hb, hb)
        source = own_states.at[kind, part] if hop == 0 else states.at[kind, hop - 1, part]
        return pltpu.make_async_remote_copy(
            src_ref=source,
            dst_ref=states.at[kind, hop, part],
            send_sem=state_send.at[kind, hop, c],
            recv_sem=state_recv.at[kind, hop, c],
            device_id={"seq": me + (1, -1)[kind]},
            device_id_type=pl.DeviceIdType.MESH,
        )

    def stat_copy(hop, c):
        part = pl.ds(c * hb, hb)
        source = own_stats.at[part] if hop == 0 else stats.at[hop - 1, part]
        return pltpu.make_async_remote_copy(
            src_ref=source,
            dst_ref=stats.at[hop, part],
            send_sem=stat_send.at[hop, c],
            recv_sem=stat_recv.at[hop, c],
            device_id={"seq": me - 1},
            device_id_type=pl.DeviceIdType.MESH,
        )

    def ids_copy(kind, hop):
        return pltpu.make_async_remote_copy(
            src_ref=ids_row if hop == 0 else ids_slots.at[kind, hop - 1],
            dst_ref=ids_slots.at[kind, hop],
            send_sem=ids_send.at[kind, hop],
            recv_sem=ids_recv.at[kind, hop],
            device_id={"seq": me + (1, -1)[kind]},
            device_id_type=pl.DeviceIdType.MESH,
        )

    def start_wide(hop, c):
        for way, kinds in ((1, (0, 1)), (-1, (2, 3))):

            @pl.when(sends(way, hop))
            def _():
                for kind in kinds:
                    wide_copy(kind, hop, c).start()

    def start_states(hop, c):
        for kind, way in enumerate((1, -1)):

            @pl.when(sends(way, hop))
            def _():
                state_copy(kind, hop, c).start()

    def await_chunk(hop, c):
        for way, kinds in ((1, (0, 1)), (-1, (2, 3))):

            @pl.when(takes(way, hop))
            def _():
                for kind in kinds:
                    wide_copy(kind, hop, c).wait_recv()
                state_copy(0 if way > 0 else 1, hop, c).wait_recv()

    ids = ids_col[...]
    pos = lax.broadcasted_iota(jnp.int32, (rows, width), 0).astype(F32)
    lane = lax.broadcasted_iota(jnp.int32, (rows, width), 1)
    head_on = jnp.where(ids == ids_col[0:1, :], 0.0, NEG)
    tail_on = jnp.where(ids == ids_col[rows - 1 : rows, :], 0.0, NEG)

    def make_states(c):
        for j in range(hb):
            h = c * hb + j
            lam = decay[h]
            cols = col(h, width)
            to_end = jnp.exp(tail_on - lam * (rows - 1.0 - pos))
            since = jnp.exp(head_on - lam * (pos + 1.0))
            kd = (lk[:, cols].astype(F32) * to_end).astype(BF16)
            qd = (lq[:, cols].astype(F32) * since).astype(BF16)
            own_states[0, h] = mm(kd, lv[:, cols], 0, 0).astype(BF16)
            own_states[1, h] = mm(qd, lg[:, cols], 0, 0).astype(BF16)

    def light(c):
        for j in range(hb):
            h = c * hb + j
            lam = decay[h]
            cols = col(h, width)
            qh, kh, vh, gh = lq[:, cols], lk[:, cols], lv[:, cols], lg[:, cols]
            state = later = None
            for d in range(reach):
                keep = jnp.exp(jnp.zeros((1, width), F32) - lam * (rows * d))
                met = ids_slots[0, d, :, rows - 1 : rows] == ids_col[0:1, :]
                left = ids_slots[1, d, :, 0:1] == ids_col[rows - 1 : rows, :]
                ahead = jnp.where(met, keep, 0.0) * states[0, d, h].astype(F32)
                back = jnp.where(left, keep, 0.0) * states[1, d, h].astype(F32)
                state = ahead if state is None else state + ahead
                later = back if later is None else later + back
            state, later = state.astype(BF16), later.astype(BF16)
            to_end = jnp.exp(tail_on - lam * (rows - 1.0 - pos))
            since = jnp.exp(head_on - lam * (pos + 1.0))
            weight = jnp.exp(bias_q[0] - lam * dist[...])
            scores = (mm(qh, kh, 1, 1) * weight).astype(BF16)
            grads = (mm(gh, vh, 1, 1) * weight).astype(BF16)
            l_out[:, cols] = (mm(scores, vh, 1, 0) + mm(qh, state, 1, 0) * since).astype(BF16)
            l_dq[:, cols] = (mm(grads, kh, 1, 0) + mm(gh, state, 1, 1) * since).astype(BF16)
            l_dk[:, cols] = (mm(grads, qh, 0, 0) + mm(vh, later, 1, 1) * to_end).astype(BF16)
            l_dv[:, cols] = (mm(scores, gh, 0, 0) + mm(kh, later, 1, 0) * to_end).astype(BF16)

    def queries(c):
        for j in range(hb):
            h = c * hb + j
            cols = col(h, width)
            qh, gh = sq[:, cols], sg[:, cols]
            keys = [sk[:, cols]] + [slots[0, d, :, cols] for d in range(reach)]
            values = [sv[:, cols]] + [slots[1, d, :, cols] for d in range(reach)]
            raw = [mm(qh, kh, 1, 1) + bias_q[d] for d, kh in enumerate(keys)]
            top = functools.reduce(jnp.maximum, raw).max(axis=1, keepdims=True)
            expo = [jnp.exp2((r - top) * unit) for r in raw]
            total = functools.reduce(jnp.add, expo).sum(axis=1, keepdims=True)
            acc = functools.reduce(
                jnp.add, [mm(e.astype(BF16), vh, 1, 0) for e, vh in zip(expo, values)]
            )
            inv = 1.0 / total
            o16 = (acc * inv).astype(BF16)
            s_out[:, cols] = o16
            delta = (gh.astype(F32) * o16.astype(F32)).sum(axis=1, keepdims=True)
            lse = top + jnp.log(total) * (1.0 / scale)
            acc = None
            for e, kh, vh in zip(expo, keys, values):
                ds = ((e * inv) * (mm(gh, vh, 1, 1) - delta)).astype(BF16)
                part = mm(ds, kh, 1, 0)
                acc = part if acc is None else acc + part
            s_dq[:, cols] = (acc * scale).astype(BF16)
            own_stats[h] = jnp.where(lane == 0, lse, delta).T[0:2, :]

    def keys_side(c):
        for j in range(hb):
            h = c * hb + j
            cols = col(h, width)
            kh, vh = sk[:, cols], sv[:, cols]
            dk_acc = dv_acc = None
            for d in range(reach + 1):
                qh = sq[:, cols] if d == 0 else slots[2, d - 1, :, cols]
                gh = sg[:, cols] if d == 0 else slots[3, d - 1, :, cols]
                st = own_stats[h] if d == 0 else stats[d - 1, h]
                lse, delta = st[0:1, :], st[1:2, :]
                raw = mm(kh, qh, 1, 1) + bias_k[d]
                prob = jnp.exp2((raw - lse) * unit)
                ds = (prob * (mm(vh, gh, 1, 1) - delta)).astype(BF16)
                dv_part = mm(prob.astype(BF16), gh, 1, 0)
                dk_part = mm(ds, qh, 1, 0)
                dk_acc = dk_part if dk_acc is None else dk_acc + dk_part
                dv_acc = dv_part if dv_acc is None else dv_acc + dv_part
            s_dk[:, cols] = (dk_acc * scale).astype(BF16)
            s_dv[:, cols] = dv_acc.astype(BF16)

    barrier = pltpu.get_barrier_semaphore()
    for way, there in ((-1, me >= 1), (1, me + 1 < shards)):

        @pl.when(there)
        def _():
            pl.semaphore_signal(
                barrier, 1, device_id={"seq": me + way}, device_id_type=pl.DeviceIdType.MESH
            )

    pl.semaphore_wait(barrier, jnp.where((me == 0) | (me == shards - 1), 1, 2))

    for kind, way in enumerate((1, -1)):

        @pl.when(sends(way, 0))
        def _():
            ids_copy(kind, 0).start()

    start_wide(0, 0)
    make_states(0)
    start_states(0, 0)

    for d in range(reach):
        for way, kinds in ((1, (0, 1)), (-1, (2, 3))):

            @pl.when(jnp.logical_not(takes(way, d)))
            def _():
                for kind in kinds:
                    slots[kind, d] = jnp.zeros((rows, all_cols), BF16)
                one = kinds[0] // 2
                states[one, d] = jnp.zeros((heads, width, width), BF16)
                ids_slots[one, d] = jnp.zeros((1, rows), jnp.int32)
                if way < 0:
                    stats[d] = jnp.zeros((heads, 2, rows), F32)

    t = lax.broadcasted_iota(jnp.int32, (rows, rows), 0)
    s = lax.broadcasted_iota(jnp.int32, (rows, rows), 1)
    same = ids == ids_row[...]
    bias_q[0] = jnp.where(same & (s <= t), 0.0, NEG)
    bias_k[0] = jnp.where(same & (t <= s), 0.0, NEG)
    dist[...] = jnp.maximum(t - s, 0).astype(F32)
    for d in range(reach):
        for kind, way in enumerate((1, -1)):

            @pl.when(takes(way, d))
            def _():
                ids_copy(kind, d).wait_recv()

            if d + 1 < reach:

                @pl.when(sends(way, d + 1))
                def _():
                    ids_copy(kind, d + 1).start()

    for d in range(reach):
        bias_q[d + 1] = jnp.where(ids == ids_slots[0, d], 0.0, NEG)
        bias_k[d + 1] = jnp.where(ids == ids_slots[1, d], 0.0, NEG)

    def step(at, carry):
        @pl.when(at + 1 < chunks)
        def _():
            start_wide(0, at + 1)
            make_states(at + 1)
            start_states(0, at + 1)

        for d in range(reach - 1):

            @pl.when((at >= d) & (at - d < chunks))
            def _():
                await_chunk(d, at - d)
                start_wide(d + 1, at - d)
                start_states(d + 1, at - d)

        mid = at - (reach - 1)

        @pl.when((mid >= 0) & (mid < chunks))
        def _():
            await_chunk(reach - 1, mid)
            queries(mid)

            @pl.when(sends(-1, 0))
            def _():
                stat_copy(0, mid).start()

            light(mid)

        for d in range(reach - 1):

            @pl.when((mid >= d) & (mid - d < chunks))
            def _():
                @pl.when(takes(-1, d))
                def _():
                    stat_copy(d, mid - d).wait_recv()

                @pl.when(sends(-1, d + 1))
                def _():
                    stat_copy(d + 1, mid - d).start()

        last = mid - (reach - 1)

        @pl.when((last >= 0) & (last < chunks))
        def _():
            @pl.when(takes(-1, reach - 1))
            def _():
                stat_copy(reach - 1, last).wait_recv()

            keys_side(last)

        return carry

    lax.fori_loop(0, chunks + 2 * (reach - 1), step, 0)

    for hop in range(reach):
        for way, kinds in ((1, (0, 1)), (-1, (2, 3))):

            @pl.when(sends(way, hop))
            def _():
                one = kinds[0] // 2
                ids_copy(one, hop).wait_send()

                def drain(c, carry):
                    for kind in kinds:
                        wide_copy(kind, hop, c).wait_send()
                    state_copy(one, hop, c).wait_send()
                    if way < 0:
                        stat_copy(hop, c).wait_send()
                    return carry

                lax.fori_loop(0, chunks, drain, 0)


def hand_out_kernel(*refs):
    sem = refs[-1]
    half = (len(refs) - 1) // 2
    copies = [pltpu.make_async_copy(refs[i], refs[half + i], sem.at[i]) for i in range(half)]
    for copy in copies:
        copy.start()
    for copy in copies:
        copy.wait()


def per_device(doc_ids, light_q, light_k, light_v, light_decay, light_grad_out, *soft):
    rows, cols = light_q.shape
    heads = light_decay.shape[0]
    width = cols // heads
    shards = lax.axis_size("seq")
    total_rows = rows * shards
    reach = min(shards - 1, (rows + total_rows // 2 - 2) // rows)
    hb = 2 if heads % 2 == 0 else 1
    chunks = heads // hb
    ids = doc_ids + 1
    vmem = pl.BlockSpec(memory_space=pltpu.VMEM)
    dma = pltpu.SemaphoreType.DMA
    done = pl.pallas_call(
        functools.partial(attention_kernel, shards, reach, heads, hb),
        in_specs=[pl.BlockSpec(memory_space=pltpu.SMEM)] + [vmem] * 10,
        out_specs=[vmem] * 8,
        out_shape=[jax.ShapeDtypeStruct((rows, cols), BF16)] * 8,
        scratch_shapes=[
            pltpu.VMEM((4, reach, rows, cols), BF16),
            pltpu.VMEM((2, reach, heads, width, width), BF16),
            pltpu.VMEM((2, heads, width, width), BF16),
            pltpu.VMEM((reach, heads, 2, rows), F32),
            pltpu.VMEM((heads, 2, rows), F32),
            pltpu.VMEM((2, reach, 1, rows), jnp.int32),
            pltpu.VMEM((reach + 1, rows, rows), F32),
            pltpu.VMEM((reach + 1, rows, rows), F32),
            pltpu.VMEM((rows, rows), F32),
            dma((4, reach, chunks)),
            dma((4, reach, chunks)),
            dma((2, reach, chunks)),
            dma((2, reach, chunks)),
            dma((reach, chunks)),
            dma((reach, chunks)),
            dma((2, reach)),
            dma((2, reach)),
        ],
        compiler_params=pltpu.CompilerParams(
            vmem_limit_bytes=VMEM_LIMIT, collective_id=0, has_side_effects=True
        ),
        cost_estimate=pl.CostEstimate(
            flops=40 * (reach + 1) * rows * rows * cols,
            bytes_accessed=32 * rows * cols,
            transcendentals=0,
        ),
        name="attention",
    )(light_decay, ids[:, None], ids[None, :], light_q, light_k, light_v, light_grad_out, *soft)
    anywhere = pl.BlockSpec(memory_space=pl.ANY)
    return pl.pallas_call(
        hand_out_kernel,
        in_specs=[anywhere] * 8,
        out_specs=[anywhere] * 8,
        out_shape=[jax.ShapeDtypeStruct((rows, cols), BF16)] * 8,
        scratch_shapes=[dma((8,))],
        cost_estimate=pl.CostEstimate(
            flops=0, bytes_accessed=32 * rows * cols, transcendentals=0
        ),
        name="hand_out",
    )(*done)


def solution(mesh):
    wide = P(("dp", "seq"), "head")
    return jax.shard_map(
        per_device,
        mesh=mesh,
        in_specs=(P(("dp", "seq")), wide, wide, wide, P("head"), wide, wide, wide, wide, wide),
        out_specs=(wide,) * 8,
        check_vma=False,
    )
```

```python
import functools
import math

import jax
import jax.numpy as jnp
from jax import lax
from jax.experimental import pallas as pl
from jax.experimental.pallas import tpu as pltpu
from jax.sharding import PartitionSpec as P

NEG = -1e30
F32 = jnp.float32
BF16 = jnp.bfloat16
VMEM_LIMIT = 60 * 1024 * 1024


def mm(a, b, ca, cb):
    return lax.dot_general(a, b, (((ca,), (cb,)), ((), ())), preferred_element_type=F32)


def attention_kernel(
    shards,
    reach,
    heads,
    hb,
    decay,
    ids_col,
    ids_row,
    lq,
    lk,
    lv,
    lg,
    sq,
    sk,
    sv,
    sg,
    l_out,
    l_dq,
    l_dk,
    l_dv,
    s_out,
    s_dq,
    s_dk,
    s_dv,
    slots,
    states,
    own_states,
    stats,
    own_stats,
    ids_slots,
    bias_q,
    bias_k,
    dist,
    send_sem,
    recv_sem,
    state_send,
    state_recv,
    stat_send,
    stat_recv,
    ids_send,
    ids_recv,
):
    rows, all_cols = lq.shape
    width = all_cols // heads
    chunks = heads // hb
    cw = hb * width
    me = lax.axis_index("seq")
    scale = width ** -0.5
    unit = scale * math.log2(math.e)
    wide_own = (sk, sv, sq, sg)
    way_of = (1, 1, -1, -1)

    def col(c, n=None):
        n = cw if n is None else n
        return pl.ds(pl.multiple_of(c * n, n), n)

    def sends(way, hop):
        if way > 0:
            return (me >= hop) & (me + 1 < shards)
        return (me + hop < shards) & (me >= 1)

    def takes(way, hop):
        return me >= hop + 1 if way > 0 else me + hop + 1 < shards

    def wide_copy(kind, hop, c):
        source = wide_own[kind].at[:, col(c)] if hop == 0 else slots.at[kind, hop - 1, :, col(c)]
        return pltpu.make_async_remote_copy(
            src_ref=source,
            dst_ref=slots.at[kind, hop, :, col(c)],
            send_sem=send_sem.at[kind, hop, c],
            recv_sem=recv_sem.at[kind, hop, c],
            device_id={"seq": me + way_of[kind]},
            device_id_type=pl.DeviceIdType.MESH,
        )

    def state_copy(kind, hop, c):
        part = pl.ds(c * hb, hb)
        source = own_states.at[kind, part] if hop == 0 else states.at[kind, hop - 1, part]
        return pltpu.make_async_remote_copy(
            src_ref=source,
            dst_ref=states.at[kind, hop, part],
            send_sem=state_send.at[kind, hop, c],
            recv_sem=state_recv.at[kind, hop, c],
            device_id={"seq": me + (1, -1)[kind]},
            device_id_type=pl.DeviceIdType.MESH,
        )

    def stat_copy(hop, c):
        part = pl.ds(c * hb, hb)
        source = own_stats.at[part] if hop == 0 else stats.at[hop - 1, part]
        return pltpu.make_async_remote_copy(
            src_ref=source,
            dst_ref=stats.at[hop, part],
            send_sem=stat_send.at[hop, c],
            recv_sem=stat_recv.at[hop, c],
            device_id={"seq": me - 1},
            device_id_type=pl.DeviceIdType.MESH,
        )

    def ids_copy(kind, hop):
        return pltpu.make_async_remote_copy(
            src_ref=ids_row if hop == 0 else ids_slots.at[kind, hop - 1],
            dst_ref=ids_slots.at[kind, hop],
            send_sem=ids_send.at[kind, hop],
            recv_sem=ids_recv.at[kind, hop],
            device_id={"seq": me + (1, -1)[kind]},
            device_id_type=pl.DeviceIdType.MESH,
        )

    def start_wide(hop, c):
        for way, kinds in ((1, (0, 1)), (-1, (2, 3))):

            @pl.when(sends(way, hop))
            def _():
                for kind in kinds:
                    wide_copy(kind, hop, c).start()

    def start_states(hop, c):
        for kind, way in enumerate((1, -1)):

            @pl.when(sends(way, hop))
            def _():
                state_copy(kind, hop, c).start()

    def await_chunk(hop, c):
        for way, kinds in ((1, (0, 1)), (-1, (2, 3))):

            @pl.when(takes(way, hop))
            def _():
                for kind in kinds:
                    wide_copy(kind, hop, c).wait_recv()
                state_copy(0 if way > 0 else 1, hop, c).wait_recv()

    ids = ids_col[...]
    pos = lax.broadcasted_iota(jnp.int32, (rows, width), 0).astype(F32)
    lane = lax.broadcasted_iota(jnp.int32, (rows, width), 1)
    head_on = jnp.where(ids == ids_col[0:1, :], 0.0, NEG)
    tail_on = jnp.where(ids == ids_col[rows - 1 : rows, :], 0.0, NEG)

    def make_states(c):
        for j in range(hb):
            h = c * hb + j
            lam = decay[h]
            cols = col(h, width)
            to_end = jnp.exp(tail_on - lam * (rows - 1.0 - pos))
            since = jnp.exp(head_on - lam * (pos + 1.0))
            kd = (lk[:, cols].astype(F32) * to_end).astype(BF16)
            qd = (lq[:, cols].astype(F32) * since).astype(BF16)
            own_states[0, h] = mm(kd, lv[:, cols], 0, 0).astype(BF16)
            own_states[1, h] = mm(qd, lg[:, cols], 0, 0).astype(BF16)

    def light(c):
        for j in range(hb):
            h = c * hb + j
            lam = decay[h]
            cols = col(h, width)
            qh, kh, vh, gh = lq[:, cols], lk[:, cols], lv[:, cols], lg[:, cols]
            state = later = None
            for d in range(reach):
                keep = jnp.exp(jnp.zeros((1, width), F32) - lam * (rows * d))
                met = ids_slots[0, d, :, rows - 1 : rows] == ids_col[0:1, :]
                left = ids_slots[1, d, :, 0:1] == ids_col[rows - 1 : rows, :]
                ahead = jnp.where(met, keep, 0.0) * states[0, d, h].astype(F32)
                back = jnp.where(left, keep, 0.0) * states[1, d, h].astype(F32)
                state = ahead if state is None else state + ahead
                later = back if later is None else later + back
            state, later = state.astype(BF16), later.astype(BF16)
            to_end = jnp.exp(tail_on - lam * (rows - 1.0 - pos))
            since = jnp.exp(head_on - lam * (pos + 1.0))
            weight = jnp.exp(bias_q[0] - lam * dist[...])
            scores = (mm(qh, kh, 1, 1) * weight).astype(BF16)
            grads = (mm(gh, vh, 1, 1) * weight).astype(BF16)
            l_out[:, cols] = (mm(scores, vh, 1, 0) + mm(qh, state, 1, 0) * since).astype(BF16)
            l_dq[:, cols] = (mm(grads, kh, 1, 0) + mm(gh, state, 1, 1) * since).astype(BF16)
            l_dk[:, cols] = (mm(grads, qh, 0, 0) + mm(vh, later, 1, 1) * to_end).astype(BF16)
            l_dv[:, cols] = (mm(scores, gh, 0, 0) + mm(kh, later, 1, 0) * to_end).astype(BF16)

    def queries(c):
        for j in range(hb):
            h = c * hb + j
            cols = col(h, width)
            qh, gh = sq[:, cols], sg[:, cols]
            keys = [sk[:, cols]] + [slots[0, d, :, cols] for d in range(reach)]
            values = [sv[:, cols]] + [slots[1, d, :, cols] for d in range(reach)]
            raw = [mm(qh, kh, 1, 1) + bias_q[d] for d, kh in enumerate(keys)]
            top = functools.reduce(jnp.maximum, raw).max(axis=1, keepdims=True)
            expo = [jnp.exp2((r - top) * unit) for r in raw]
            total = functools.reduce(jnp.add, expo).sum(axis=1, keepdims=True)
            acc = functools.reduce(
                jnp.add, [mm(e.astype(BF16), vh, 1, 0) for e, vh in zip(expo, values)]
            )
            inv = 1.0 / total
            o16 = (acc * inv).astype(BF16)
            s_out[:, cols] = o16
            delta = (gh.astype(F32) * o16.astype(F32)).sum(axis=1, keepdims=True)
            lse = top + jnp.log(total) * (1.0 / scale)
            acc = None
            for e, kh, vh in zip(expo, keys, values):
                ds = ((e * inv) * (mm(gh, vh, 1, 1) - delta)).astype(BF16)
                part = mm(ds, kh, 1, 0)
                acc = part if acc is None else acc + part
            s_dq[:, cols] = (acc * scale).astype(BF16)
            own_stats[h] = jnp.where(lane == 0, lse, delta).T[0:2, :]

    def keys_side(c):
        for j in range(hb):
            h = c * hb + j
            cols = col(h, width)
            kh, vh = sk[:, cols], sv[:, cols]
            dk_acc = dv_acc = None
            for d in range(reach + 1):
                qh = sq[:, cols] if d == 0 else slots[2, d - 1, :, cols]
                gh = sg[:, cols] if d == 0 else slots[3, d - 1, :, cols]
                st = own_stats[h] if d == 0 else stats[d - 1, h]
                lse, delta = st[0:1, :], st[1:2, :]
                raw = mm(kh, qh, 1, 1) + bias_k[d]
                prob = jnp.exp2((raw - lse) * unit)
                ds = (prob * (mm(vh, gh, 1, 1) - delta)).astype(BF16)
                dv_part = mm(prob.astype(BF16), gh, 1, 0)
                dk_part = mm(ds, qh, 1, 0)
                dk_acc = dk_part if dk_acc is None else dk_acc + dk_part
                dv_acc = dv_part if dv_acc is None else dv_acc + dv_part
            s_dk[:, cols] = (dk_acc * scale).astype(BF16)
            s_dv[:, cols] = dv_acc.astype(BF16)

    barrier = pltpu.get_barrier_semaphore()
    for way, there in ((-1, me >= 1), (1, me + 1 < shards)):

        @pl.when(there)
        def _():
            pl.semaphore_signal(
                barrier, 1, device_id={"seq": me + way}, device_id_type=pl.DeviceIdType.MESH
            )

    pl.semaphore_wait(barrier, jnp.where((me == 0) | (me == shards - 1), 1, 2))

    for kind, way in enumerate((1, -1)):

        @pl.when(sends(way, 0))
        def _():
            ids_copy(kind, 0).start()

    start_wide(0, 0)
    make_states(0)
    start_states(0, 0)

    for d in range(reach):
        for way, kinds in ((1, (0, 1)), (-1, (2, 3))):

            @pl.when(jnp.logical_not(takes(way, d)))
            def _():
                for kind in kinds:
                    slots[kind, d] = jnp.zeros((rows, all_cols), BF16)
                one = kinds[0] // 2
                states[one, d] = jnp.zeros((heads, width, width), BF16)
                ids_slots[one, d] = jnp.zeros((1, rows), jnp.int32)
                if way < 0:
                    stats[d] = jnp.zeros((heads, 2, rows), F32)

    t = lax.broadcasted_iota(jnp.int32, (rows, rows), 0)
    s = lax.broadcasted_iota(jnp.int32, (rows, rows), 1)
    same = ids == ids_row[...]
    bias_q[0] = jnp.where(same & (s <= t), 0.0, NEG)
    bias_k[0] = jnp.where(same & (t <= s), 0.0, NEG)
    dist[...] = jnp.maximum(t - s, 0).astype(F32)
    for d in range(reach):
        for kind, way in enumerate((1, -1)):

            @pl.when(takes(way, d))
            def _():
                ids_copy(kind, d).wait_recv()

            if d + 1 < reach:

                @pl.when(sends(way, d + 1))
                def _():
                    ids_copy(kind, d + 1).start()

    for d in range(reach):
        bias_q[d + 1] = jnp.where(ids == ids_slots[0, d], 0.0, NEG)
        bias_k[d + 1] = jnp.where(ids == ids_slots[1, d], 0.0, NEG)

    def step(at, carry):
        @pl.when(at + 1 < chunks)
        def _():
            start_wide(0, at + 1)
            make_states(at + 1)
            start_states(0, at + 1)

        for d in range(reach - 1):

            @pl.when((at >= d) & (at - d < chunks))
            def _():
                await_chunk(d, at - d)
                start_wide(d + 1, at - d)
                start_states(d + 1, at - d)

        mid = at - (reach - 1)

        @pl.when((mid >= 0) & (mid < chunks))
        def _():
            await_chunk(reach - 1, mid)
            queries(mid)

            @pl.when(sends(-1, 0))
            def _():
                stat_copy(0, mid).start()

            light(mid)

        for d in range(reach - 1):

            @pl.when((mid >= d) & (mid - d < chunks))
            def _():
                @pl.when(takes(-1, d))
                def _():
                    stat_copy(d, mid - d).wait_recv()

                @pl.when(sends(-1, d + 1))
                def _():
                    stat_copy(d + 1, mid - d).start()

        last = mid - (reach - 1)

        @pl.when((last >= 0) & (last < chunks))
        def _():
            @pl.when(takes(-1, reach - 1))
            def _():
                stat_copy(reach - 1, last).wait_recv()

            keys_side(last)

        return carry

    lax.fori_loop(0, chunks + 2 * (reach - 1), step, 0)

    for hop in range(reach):
        for way, kinds in ((1, (0, 1)), (-1, (2, 3))):

            @pl.when(sends(way, hop))
            def _():
                one = kinds[0] // 2
                ids_copy(one, hop).wait_send()

                def drain(c, carry):
                    for kind in kinds:
                        wide_copy(kind, hop, c).wait_send()
                    state_copy(one, hop, c).wait_send()
                    if way < 0:
                        stat_copy(hop, c).wait_send()
                    return carry

                lax.fori_loop(0, chunks, drain, 0)


def hand_out_kernel(*refs):
    half = len(refs) // 2
    for i in range(half):
        refs[half + i][...] = refs[i][...]


def per_device(doc_ids, light_q, light_k, light_v, light_decay, light_grad_out, *soft):
    rows, cols = light_q.shape
    heads = light_decay.shape[0]
    width = cols // heads
    shards = lax.axis_size("seq")
    total_rows = rows * shards
    reach = min(shards - 1, (rows + total_rows // 2 - 2) // rows)
    hb = 2 if heads % 2 == 0 else 1
    chunks = heads // hb
    ids = doc_ids + 1
    vmem = pl.BlockSpec(memory_space=pltpu.VMEM)
    dma = pltpu.SemaphoreType.DMA
    done = pl.pallas_call(
        functools.partial(attention_kernel, shards, reach, heads, hb),
        in_specs=[pl.BlockSpec(memory_space=pltpu.SMEM)] + [vmem] * 10,
        out_specs=[vmem] * 8,
        out_shape=[jax.ShapeDtypeStruct((rows, cols), BF16)] * 8,
        scratch_shapes=[
            pltpu.VMEM((4, reach, rows, cols), BF16),
            pltpu.VMEM((2, reach, heads, width, width), BF16),
            pltpu.VMEM((2, heads, width, width), BF16),
            pltpu.VMEM((reach, heads, 2, rows), F32),
            pltpu.VMEM((heads, 2, rows), F32),
            pltpu.VMEM((2, reach, 1, rows), jnp.int32),
            pltpu.VMEM((reach + 1, rows, rows), F32),
            pltpu.VMEM((reach + 1, rows, rows), F32),
            pltpu.VMEM((rows, rows), F32),
            dma((4, reach, chunks)),
            dma((4, reach, chunks)),
            dma((2, reach, chunks)),
            dma((2, reach, chunks)),
            dma((reach, chunks)),
            dma((reach, chunks)),
            dma((2, reach)),
            dma((2, reach)),
        ],
        compiler_params=pltpu.CompilerParams(
            vmem_limit_bytes=VMEM_LIMIT, collective_id=0, has_side_effects=True
        ),
        cost_estimate=pl.CostEstimate(
            flops=40 * (reach + 1) * rows * rows * cols,
            bytes_accessed=32 * rows * cols,
            transcendentals=0,
        ),
        name="attention",
    )(light_decay, ids[:, None], ids[None, :], light_q, light_k, light_v, light_grad_out, *soft)
    piece = pl.BlockSpec((rows // 4, cols), lambda i: (i, 0))
    return pl.pallas_call(
        hand_out_kernel,
        grid=(4,),
        in_specs=[piece] * 8,
        out_specs=[piece] * 8,
        out_shape=[jax.ShapeDtypeStruct((rows, cols), BF16)] * 8,
        compiler_params=pltpu.CompilerParams(vmem_limit_bytes=VMEM_LIMIT),
        cost_estimate=pl.CostEstimate(
            flops=0, bytes_accessed=32 * rows * cols, transcendentals=0
        ),
        name="hand_out",
    )(*done)


def solution(mesh):
    wide = P(("dp", "seq"), "head")
    return jax.shard_map(
        per_device,
        mesh=mesh,
        in_specs=(P(("dp", "seq")), wide, wide, wide, P("head"), wide, wide, wide, wide, wide),
        out_specs=(wide,) * 8,
        check_vma=False,
    )
```
